32 devices in a mesh: shot: 2 (over x), gx: 16 (over z, y, core).
Axes of the slice: x: 2, y: 2, z: 4, core: 2. Of those that a mesh axis runs over, the one named last changes fastest.
Arguments:
- adjoint_now: float32 [32, 16, 32, 128], P(('shot', 'gx')), parts along dimension 0, may hold values from -6 to 6
- adjoint_before: float32 [32, 16, 32, 128], P(('shot', 'gx')), parts along dimension 0, may hold values from -6 to 6
- vel_coeff: float32 [16, 16, 32, 128], P('gx'), may hold values from 0.04 to 0.18
- forward_accel: bfloat16 [8, 16, 16, 32, 128], P('shot', 'gx'), parts along dimension 0, may hold values from -6 to 6
- residual: float32 [8, 32768], P('shot', 'gx'), parts along dimension 0, may hold values from -6 to 6
- rec_cell: int32 [32768], P('gx'), may hold values from 0 to 65535
- owner_list: int32 [256, 384], P('gx'), may hold values from -1 to 2047, as said below
- trace_count: int32 [32], P(('shot', 'gx')), parts along dimension 0, may hold values from 1024 to 2048, as said below
Outputs:
- adjoint_final: float32 [32, 16, 32, 128], P(('shot', 'gx')), parts along dimension 0
- adjoint_prior: float32 [32, 16, 32, 128], P(('shot', 'gx')), parts along dimension 0
- gradient: float32 [32, 16, 32, 128], P(('shot', 'gx')), parts along dimension 0
The draws below stay inside these ranges and needn't reach their ends.
There are 2 independent parts, one for each index of `shot`. The reference program is written for one: setup_inputs(seed, part) draws one part's arguments, and reference() takes and returns one part's arrays. A program takes and returns all parts, laid end to end along the dimension named above; an argument that names none is the same for every part. Nothing has to cross between parts.
Inputs may be any that keep to these rules, and one draw needn't show every extreme that they name: `owner_list`: row d * 16 + e holds in some of its 384 slots the local indices of device d's traces owned by pencil e, and -1 in the other slots; each local index 0 to 2047 of a device stands exactly once in that device's 16 rows. Traces 0 to trace_count[d] - 1 of device d are live; the others carry no source.
All inputs are finite; a program needn't handle non-finite values.
Results may differ from the reference program's by a relative error of at most 0.0003.
Values sent between devices are 32-bit elements; how exact they have to be, the bound alone decides.
A program may use at most 256 MiB of HBM per device.

```python
import math
import jax
import jax.numpy as jnp
from jax import lax

PY = 4
CX = 16
CY = 32
NZ = 128
TR_DEV = 2048
STEPS = 4
TRACES = 32768
CAP = 384
CELLS = 65536
N_GX = 16


def draw_owner_list(key, part):
    key = jax.random.fold_in(key, 11)
    shuffle_key, random_key = jax.random.split(key)
    device_count = TRACES // TR_DEV
    slot_total = device_count * CAP
    owner_ids = jnp.arange(slot_total, dtype=jnp.int32) // CAP
    shuffled = jax.random.permutation(shuffle_key, device_count)
    favoured = (owner_ids == shuffled[0]) | (owner_ids == shuffled[1])
    random_part = jax.random.randint(random_key, (device_count, slot_total), 0, 4096)
    scores = (random_part + jnp.where(favoured, 4096, 0)[None, :]) * slot_total + jnp.arange(slot_total, dtype=jnp.int32)[None, :]
    scores_top, chosen = lax.top_k(scores, TR_DEV)
    device_base = jnp.arange(device_count, dtype=jnp.int32)[:, None] * slot_total
    flat_slot = (chosen.astype(jnp.int32) + device_base).reshape(-1)
    local_ids = jnp.broadcast_to(jnp.arange(TR_DEV, dtype=jnp.int32)[None, :], (device_count, TR_DEV)).reshape(-1)
    lists = jnp.full((device_count * slot_total,), -1, jnp.int32).at[flat_slot].set(local_ids)
    return lists.reshape(device_count * device_count, CAP)


def draw_trace_count(key, part):
    key = jax.random.fold_in(key, 23)
    count_key, order_key = jax.random.split(key)
    device_count = TRACES // TR_DEV
    counts = jax.random.randint(count_key, (device_count,), TR_DEV // 2, TR_DEV + 1)
    order = jax.random.permutation(order_key, device_count)
    device_ids = jnp.arange(device_count, dtype=jnp.int32)
    counts = jnp.where(device_ids == order[0], TR_DEV, counts)
    counts = jnp.where(device_ids == order[1], TR_DEV // 2, counts)
    return counts.astype(jnp.int32)


def place_ends(result, stream_key, low, largest):
    longest = result.shape.index(max(result.shape))
    spots = []
    for shift in (0, 1):
        where = [jax.random.randint(jax.random.fold_in(stream_key, axis), (), 0, length) for axis, length in enumerate(result.shape)]
        where[longest] = (where[longest] + shift) % result.shape[longest]
        spots.append(tuple(where))
    return result.at[spots[0]].set(low).at[spots[1]].set(largest)


def levels(stream_key, dims, shards, low, largest):
    def one(dim, shards_of):
        draws = jax.random.uniform(jax.random.fold_in(jax.random.fold_in(stream_key, 6), dim), (shards_of,), jnp.float32, low / len(shards), largest / len(shards))
        return jnp.repeat(jnp.exp(draws), dims[dim] // shards_of).reshape((-1,) + (1,) * (len(dims) - dim - 1))

    gain = one(*shards[0])
    for cut in shards[1:]:
        gain = gain * one(*cut)
    return gain


def gaussian(stream_key, shape, spread, bound, cuts=(), kind=jnp.bfloat16):
    gain = levels(stream_key, shape, cuts, -0.22, 0.18) if cuts else 1.0
    array = jax.random.normal(stream_key, shape, jnp.float32) * spread * gain
    return jnp.minimum(jnp.maximum(array, -bound), bound).astype(kind)


def setup_inputs(seed: int = 0, part: int = 0) -> dict:
    key_of = jax.random.split(jax.random.key(seed), 9)
    own_keys = jax.random.split(jax.random.fold_in(key_of[8], part), 9)
    adjoint_now = gaussian(own_keys[0], (N_GX, CX, CY, NZ), 1.0, 6.0, ((0, 16),), jnp.float32)
    adjoint_before = gaussian(own_keys[1], (N_GX, CX, CY, NZ), 1.0, 6.0, ((0, 16),), jnp.float32)
    vel_coeff = jnp.clip(jnp.exp(math.log(0.18) - 1.50407746 * jax.random.uniform(key_of[2], (N_GX, CX, CY, NZ), jnp.float32) ** levels(key_of[2], (N_GX, CX, CY, NZ), ((0, 16),), -0.2, 0.2)), 0.04, 0.18)
    forward_accel = gaussian(own_keys[3], (STEPS, N_GX, CX, CY, NZ), 1.0, 6.0, ((1, 16),))
    residual = gaussian(own_keys[4], (STEPS, TRACES), 1.0, 6.0, ((1, 16),), jnp.float32)
    rec_cell = place_ends(jax.random.randint(key_of[5], (TRACES,), 0, CELLS), jax.random.fold_in(key_of[5], 1), 0, CELLS - 1).astype(jnp.int32)
    owner_list = draw_owner_list(jax.random.fold_in(key_of[8], 71), part)
    trace_count = draw_trace_count(jax.random.fold_in(jax.random.fold_in(key_of[8], part), 71), part)
    return {"adjoint_now": adjoint_now, "adjoint_before": adjoint_before, "vel_coeff": vel_coeff, "forward_accel": forward_accel, "residual": residual, "rec_cell": rec_cell, "owner_list": owner_list, "trace_count": trace_count}


weights = (-205.0 / 72.0, 8.0 / 5.0, -1.0 / 5.0, 8.0 / 315.0, -1.0 / 560.0)


def laplace(region):
    extent_first, extent_second, extent_third = region.shape
    padded = jnp.pad(region, 4)
    result_sum = 3.0 * weights[0] * region
    for offset in range(1, 5):
        pairs = padded[4 + offset:4 + offset + extent_first, 4:4 + extent_second, 4:4 + extent_third]
        pairs = pairs + padded[4 - offset:4 - offset + extent_first, 4:4 + extent_second, 4:4 + extent_third]
        pairs = pairs + padded[4:4 + extent_first, 4 + offset:4 + offset + extent_second, 4:4 + extent_third]
        pairs = pairs + padded[4:4 + extent_first, 4 - offset:4 - offset + extent_second, 4:4 + extent_third]
        pairs = pairs + padded[4:4 + extent_first, 4:4 + extent_second, 4 + offset:4 + offset + extent_third]
        pairs = pairs + padded[4:4 + extent_first, 4:4 + extent_second, 4 - offset:4 - offset + extent_third]
        result_sum = result_sum + weights[offset] * pairs
    return result_sum


def to_grid(blocks):
    pencils_x = N_GX // PY
    shaped = blocks.reshape(pencils_x, PY, CX, CY, NZ).transpose(0, 2, 1, 3, 4)
    return shaped.reshape(pencils_x * CX, PY * CY, NZ)


def from_grid(field):
    pencils_x = N_GX // PY
    shaped = field.reshape(pencils_x, CX, PY, CY, NZ).transpose(0, 2, 1, 3, 4)
    return shaped.reshape(N_GX, CX, CY, NZ)


def reference(adjoint_now, adjoint_before, vel_coeff, forward_accel, residual, rec_cell, owner_list, trace_count):
    cell_count = CX * CY * NZ
    entries = jnp.arange(N_GX * N_GX * CAP, dtype=jnp.int32)
    sender = entries // (N_GX * CAP)
    owner_id = (entries // CAP) % N_GX
    listed = owner_list.reshape(-1)
    filled = (listed >= 0) & (listed < trace_count[sender])
    trace_id = sender * TR_DEV + jnp.maximum(listed, 0)
    target = owner_id * cell_count + rec_cell[trace_id]
    values = jnp.where(filled[None, :], residual[:, trace_id], jnp.zeros((), residual.dtype))
    sources = jnp.zeros((STEPS, N_GX * cell_count), residual.dtype).at[:, target].add(values)
    sources = sources.reshape(STEPS, N_GX, CX, CY, NZ)
    present = to_grid(adjoint_now)
    before = to_grid(adjoint_before)
    velocity = to_grid(vel_coeff)
    gradient = jnp.zeros_like(present)
    for moment in range(STEPS):
        following = 2.0 * present - before + velocity * laplace(present) + to_grid(sources[moment])
        gradient = gradient + following * to_grid(forward_accel[moment]).astype(present.dtype)
        before = present
        present = following
    return from_grid(present), from_grid(before), from_grid(gradient)
```

```python
import functools

import jax
import jax.numpy as jnp
from jax import lax
from jax.experimental import pallas as pl
from jax.experimental.pallas import tpu as pltpu
from jax.sharding import PartitionSpec as P

PY = 4
LANES = 128
ROWS = 8
GROUP = 4

weights = (-205.0 / 72.0, 8.0 / 5.0, -1.0 / 5.0, 8.0 / 315.0, -1.0 / 560.0)


def kernel(
    n,
    now_ref,
    before_ref,
    vel_ref,
    accel_ref,
    residual_ref,
    cell_ref,
    list_ref,
    count_ref,
    final_ref,
    prior_ref,
    gradient_ref,
    table,
    packed,
    arrived,
    field,
    sources,
    halo_send,
    halo_recv,
    trace_send,
    trace_recv,
):
    steps, cx, cy, nz = accel_ref.shape
    traces = residual_ref.shape[1]
    slots = list_ref.shape[1]
    me = lax.axis_index("gx")
    spot = me % PY

    barrier = pltpu.get_barrier_semaphore()

    def greet(j, carry):
        pl.semaphore_signal(barrier, inc=1, device_id={"gx": (me + j) % n})
        return carry

    lax.fori_loop(1, n, greet, 0)

    field[0, 4 : 4 + cx, 8 : 8 + cy] = now_ref[...]

    has = (me + PY < n, me - PY >= 0, spot < PY - 1, spot > 0)
    gets = (has[1], has[0], has[3], has[2])
    target = ((me + PY) % n, (me - PY + n) % n, (me + 1) % n, (me - 1 + n) % n)
    inside_y = pl.ds(8, cy)
    inside_x = pl.ds(4, cx)
    source_of = (
        (pl.ds(cx, 4), inside_y),
        (pl.ds(4, 4), inside_y),
        (inside_x, pl.ds(cy, 8)),
        (inside_x, pl.ds(8, 8)),
    )
    place_of = (
        (pl.ds(0, 4), inside_y),
        (pl.ds(cx + 4, 4), inside_y),
        (inside_x, pl.ds(0, 8)),
        (inside_x, pl.ds(cy + 8, 8)),
    )

    def halo_copy(s, way):
        return pltpu.make_async_remote_copy(
            src_ref=field.at[(s,) + source_of[way]],
            dst_ref=field.at[(s,) + place_of[way]],
            send_sem=halo_send.at[s, way],
            recv_sem=halo_recv.at[s, way],
            device_id={"gx": target[way]},
        )

    def send_halo(s, way):
        @pl.when(has[way])
        def _():
            halo_copy(s, way).start()

    def wait_halo(s, way):
        @pl.when(gets[way])
        def _():
            halo_copy(s, way).wait_recv()

    for way in range(4):

        @pl.when(jnp.logical_not(gets[way]))
        def _():
            for s in range(steps):
                place = field.at[(s,) + place_of[way]]
                place[...] = jnp.zeros(place.shape, jnp.float32)

    table[0:steps] = residual_ref[...]
    table[steps : steps + 1] = cell_ref[...].astype(jnp.float32)
    table[steps + 1 :] = jnp.zeros((ROWS - steps - 1, traces), jnp.float32)
    count = count_ref[0]
    row = lax.broadcasted_iota(jnp.int32, (ROWS, LANES), 0)

    def pack(t, carry):
        tile = list_ref[pl.ds(pl.multiple_of(t * ROWS, ROWS), ROWS)]
        for r in range(ROWS):
            for k in range(0, slots, LANES):
                listed = jnp.broadcast_to(tile[r : r + 1, k : k + LANES], (ROWS, LANES))
                high = listed >> 7
                low = listed & (LANES - 1)
                found = jnp.zeros((ROWS, LANES), jnp.float32)
                for h in range(traces // LANES):
                    taken = jnp.take_along_axis(
                        table[:, h * LANES : (h + 1) * LANES],
                        low,
                        axis=1,
                        mode="promise_in_bounds",
                    )
                    found = jnp.where(high == h, taken, found)
                kept = (listed < count) | (row >= steps)
                packed[t * ROWS + r, :, k : k + LANES] = jnp.where(kept, found, 0.0)
        return carry

    lax.fori_loop(0, n // ROWS, pack, 0)

    pl.semaphore_wait(barrier, n - 1)

    for way in range(4):
        send_halo(0, way)

    def trace_copy(e):
        return pltpu.make_async_remote_copy(
            src_ref=packed.at[e],
            dst_ref=arrived.at[me],
            send_sem=trace_send.at[e],
            recv_sem=trace_recv.at[me],
            device_id={"gx": e},
        )

    def send_traces(j, carry):
        trace_copy((me + j) % n).start()
        return carry

    lax.fori_loop(1, n, send_traces, 0)
    arrived[me] = packed[me]

    def wait_traces(sender):
        pltpu.make_async_remote_copy(
            src_ref=packed.at[sender],
            dst_ref=arrived.at[sender],
            send_sem=trace_send.at[sender],
            recv_sem=trace_recv.at[sender],
            device_id={"gx": sender},
        ).wait_recv()

    cells = cx * cy
    span = GROUP * slots
    high_index = lax.broadcasted_iota(jnp.int32, (cells, span), 0)
    low_index = lax.broadcasted_iota(jnp.int32, (nz, span), 0)

    def inject(half):
        def add_group(g, carry):
            senders = [(me + g * GROUP + j) % n for j in range(GROUP)]
            if half == 0:
                for sender in senders:

                    @pl.when(sender != me)
                    def _():
                        wait_traces(sender)

            block = jnp.concatenate([arrived[sender] for sender in senders], axis=1)
            cell = block[steps : steps + 1].astype(jnp.int32)
            high = (cell >> 7)
            low = cell & (LANES - 1)
            ones = jnp.where(high_index == high, 1.0, 0.0).astype(jnp.bfloat16)
            at_low = low_index == low
            coarse, fine = [], []
            for s in (2 * half, 2 * half + 1):
                value = block[s : s + 1]
                top = value.astype(jnp.bfloat16).astype(jnp.float32)
                coarse.append(jnp.where(at_low, top, 0.0).astype(jnp.bfloat16))
                fine.append(jnp.where(at_low, value - top, 0.0).astype(jnp.bfloat16))
            total = 0.0
            for part in (coarse, fine):
                total += lax.dot_general(
                    ones,
                    jnp.concatenate(part, axis=0),
                    (((1,), (1,)), ((), ())),
                    preferred_element_type=jnp.float32,
                )
            for j in range(2):
                sources[2 * half + j] += total[:, j * nz : (j + 1) * nz]
            return carry

        for j in range(2):
            sources[2 * half + j] = jnp.zeros((cells, nz), jnp.float32)
        lax.fori_loop(0, n // GROUP, add_group, 0)

    lane = lax.broadcasted_iota(jnp.int32, (1, nz), 1)
    up = [jnp.where(lane >= k, weights[k], 0.0) for k in range(1, 5)]
    down = [jnp.where(lane < nz - k, weights[k], 0.0) for k in range(1, 5)]

    def advance(s, first, last):
        def plane(x, carry):
            present = field[s, x + 4, 8 : 8 + cy]
            total = 3.0 * weights[0] * present
            for k in range(1, 5):
                pairs = field[s, x + 4 + k, 8 : 8 + cy] + field[s, x + 4 - k, 8 : 8 + cy]
                pairs += field[s, x + 4, 8 + k : 8 + k + cy]
                pairs += field[s, x + 4, 8 - k : 8 - k + cy]
                total += weights[k] * pairs
                total += up[k - 1] * pltpu.roll(present, k, 1)
                total += down[k - 1] * pltpu.roll(present, nz - k, 1)
            old = before_ref[x] if s == 0 else field[s - 1, x + 4, 8 : 8 + cy]
            here = pl.ds(pl.multiple_of(x * cy, cy), cy)
            following = 2.0 * present - old + vel_ref[x] * total + sources[s, here]
            if s + 1 < steps:
                field[s + 1, x + 4, 8 : 8 + cy] = following
            else:
                final_ref[x] = following
                prior_ref[x] = present
            term = following * accel_ref[s, x].astype(jnp.float32)
            gradient_ref[x] = term if s == 0 else gradient_ref[x] + term
            return carry

        lax.fori_loop(first, last, plane, 0)

    inject(0)
    for s in range(steps):
        for way in range(4):
            wait_halo(s, way)
        advance(s, 0, 4)
        if s + 1 < steps:
            send_halo(s + 1, 1)
        advance(s, cx - 4, cx)
        if s + 1 < steps:
            send_halo(s + 1, 0)
        advance(s, 4, cx - 4)
        if s + 1 < steps:
            send_halo(s + 1, 2)
            send_halo(s + 1, 3)
        if s == 0:
            inject(1)

    def finish(j, carry):
        trace_copy((me + j) % n).wait_send()
        return carry

    lax.fori_loop(1, n, finish, 0)
    for s in range(steps):
        for way in range(4):

            @pl.when(has[way])
            def _():
                halo_copy(s, way).wait_send()


def per_device(
    adjoint_now,
    adjoint_before,
    vel_coeff,
    forward_accel,
    residual,
    rec_cell,
    owner_list,
    trace_count,
):
    n = lax.axis_size("gx")
    steps, _, cx, cy, nz = forward_accel.shape
    traces = residual.shape[1]
    short = -owner_list.shape[1] % LANES
    lists = owner_list
    if short:
        lists = jnp.pad(owner_list, ((0, 0), (0, short)), constant_values=-1)
    slots = lists.shape[1]
    whole = pl.BlockSpec(memory_space=pltpu.VMEM)
    shape = jax.ShapeDtypeStruct((cx, cy, nz), jnp.float32)
    final, prior, gradient = pl.pallas_call(
        functools.partial(kernel, n),
        out_shape=(shape, shape, shape),
        in_specs=[whole] * 7 + [pl.BlockSpec(memory_space=pltpu.SMEM)],
        out_specs=(whole, whole, whole),
        scratch_shapes=[
            pltpu.VMEM((ROWS, traces), jnp.float32),
            pltpu.VMEM((n, ROWS, slots), jnp.float32),
            pltpu.VMEM((n, ROWS, slots), jnp.float32),
            pltpu.VMEM((steps, cx + 8, cy + 16, nz), jnp.float32),
            pltpu.VMEM((steps, cx * cy, nz), jnp.float32),
            pltpu.SemaphoreType.DMA((steps, 4)),
            pltpu.SemaphoreType.DMA((steps, 4)),
            pltpu.SemaphoreType.DMA((n,)),
            pltpu.SemaphoreType.DMA((n,)),
        ],
        compiler_params=pltpu.CompilerParams(
            collective_id=0, has_side_effects=True, vmem_limit_bytes=48 * 1024 * 1024
        ),
    )(
        adjoint_now[0],
        adjoint_before[0],
        vel_coeff[0],
        forward_accel[:, 0],
        residual,
        rec_cell[None],
        lists,
        trace_count,
    )
    return final[None], prior[None], gradient[None]


def solution(mesh):
    in_specs = (
        P(("shot", "gx"), None, None, None),
        P(("shot", "gx"), None, None, None),
        P("gx", None, None, None),
        P("shot", "gx", None, None, None),
        P("shot", "gx"),
        P("gx"),
        P("gx", None),
        P(("shot", "gx")),
    )
    out_specs = (
        P(("shot", "gx"), None, None, None),
        P(("shot", "gx"), None, None, None),
        P(("shot", "gx"), None, None, None),
    )
    return jax.shard_map(
        per_device, mesh=mesh, in_specs=in_specs, out_specs=out_specs, check_vma=False
    )
```

```python
import functools

import jax
import jax.numpy as jnp
from jax import lax
from jax.experimental import pallas as pl
from jax.experimental.pallas import tpu as pltpu
from jax.sharding import PartitionSpec as P

PY = 4
LANES = 128
ROWS = 8
GROUP = 4
VMEM = 63 * 1024 * 1024

weights = (-205.0 / 72.0, 8.0 / 5.0, -1.0 / 5.0, 8.0 / 315.0, -1.0 / 560.0)


def kernel(
    n,
    now_hbm,
    before_hbm,
    vel_hbm,
    accel_hbm,
    residual_hbm,
    cell_hbm,
    list_hbm,
    count_ref,
    final_ref,
    prior_ref,
    gradient_ref,
    before_ref,
    vel_ref,
    accel_ref,
    residual_ref,
    cell_ref,
    list_ref,
    table,
    packed,
    arrived,
    field,
    sources,
    halo_send,
    halo_recv,
    trace_send,
    trace_recv,
    load_sem,
):
    steps, cx, cy, nz = accel_ref.shape
    traces = residual_ref.shape[1]
    slots = list_ref.shape[1]
    me = lax.axis_index("gx")
    spot = me % PY

    barrier = pltpu.get_barrier_semaphore()

    def greet(j, carry):
        pl.semaphore_signal(barrier, inc=1, device_id={"gx": (me + j) % n})
        return carry

    lax.fori_loop(1, n, greet, 0)

    loads = [
        pltpu.make_async_copy(there, here, load_sem.at[i])
        for i, (there, here) in enumerate(
            (
                (list_hbm, list_ref),
                (residual_hbm, residual_ref),
                (cell_hbm, cell_ref),
                (now_hbm, field.at[0, 4 : 4 + cx, 8 : 8 + cy]),
                (before_hbm, before_ref),
                (vel_hbm, vel_ref),
                (accel_hbm, accel_ref),
            )
        )
    ]
    for load in loads:
        load.start()

    has = (me + PY < n, me - PY >= 0, spot < PY - 1, spot > 0)
    gets = (has[1], has[0], has[3], has[2])
    target = ((me + PY) % n, (me - PY + n) % n, (me + 1) % n, (me - 1 + n) % n)
    inside_y = pl.ds(8, cy)
    inside_x = pl.ds(4, cx)
    source_of = (
        (pl.ds(cx, 4), inside_y),
        (pl.ds(4, 4), inside_y),
        (inside_x, pl.ds(cy, 8)),
        (inside_x, pl.ds(8, 8)),
    )
    place_of = (
        (pl.ds(0, 4), inside_y),
        (pl.ds(cx + 4, 4), inside_y),
        (inside_x, pl.ds(0, 8)),
        (inside_x, pl.ds(cy + 8, 8)),
    )

    def halo_copy(s, way):
        return pltpu.make_async_remote_copy(
            src_ref=field.at[(s,) + source_of[way]],
            dst_ref=field.at[(s,) + place_of[way]],
            send_sem=halo_send.at[s, way],
            recv_sem=halo_recv.at[s, way],
            device_id={"gx": target[way]},
        )

    def send_halo(s, way):
        @pl.when(has[way])
        def _():
            halo_copy(s, way).start()

    def wait_halo(s, way):
        @pl.when(gets[way])
        def _():
            halo_copy(s, way).wait_recv()

    for way in range(4):

        @pl.when(jnp.logical_not(gets[way]))
        def _():
            for s in range(steps):
                place = field.at[(s,) + place_of[way]]
                place[...] = jnp.zeros(place.shape, jnp.float32)

    loads[3].wait()
    pl.semaphore_wait(barrier, n - 1)
    for way in range(4):
        send_halo(0, way)

    for load in loads[:3]:
        load.wait()
    table[0:steps] = residual_ref[...]
    table[steps : steps + 1] = cell_ref[...].astype(jnp.float32)
    table[steps + 1 :] = jnp.zeros((ROWS - steps - 1, traces), jnp.float32)
    count = count_ref[0]
    row = lax.broadcasted_iota(jnp.int32, (ROWS, LANES), 0)

    def pack(t, carry):
        tile = list_ref[pl.ds(pl.multiple_of(t * ROWS, ROWS), ROWS)]
        for r in range(ROWS):
            for k in range(0, slots, LANES):
                listed = jnp.broadcast_to(tile[r : r + 1, k : k + LANES], (ROWS, LANES))
                high = listed >> 7
                low = listed & (LANES - 1)
                found = jnp.zeros((ROWS, LANES), jnp.float32)
                for h in range(traces // LANES):
                    taken = jnp.take_along_axis(
                        table[:, h * LANES : (h + 1) * LANES],
                        low,
                        axis=1,
                        mode="promise_in_bounds",
                    )
                    found = jnp.where(high == h, taken, found)
                kept = (listed < count) | (row >= steps)
                packed[t * ROWS + r, :, k : k + LANES] = jnp.where(kept, found, 0.0)
        return carry

    lax.fori_loop(0, n // ROWS, pack, 0)

    def trace_copy(e):
        return pltpu.make_async_remote_copy(
            src_ref=packed.at[e],
            dst_ref=arrived.at[me],
            send_sem=trace_send.at[e],
            recv_sem=trace_recv.at[me],
            device_id={"gx": e},
        )

    def send_traces(j, carry):
        trace_copy((me + j) % n).start()
        return carry

    lax.fori_loop(1, n, send_traces, 0)
    arrived[me] = packed[me]

    def wait_traces(sender):
        pltpu.make_async_remote_copy(
            src_ref=packed.at[sender],
            dst_ref=arrived.at[sender],
            send_sem=trace_send.at[sender],
            recv_sem=trace_recv.at[sender],
            device_id={"gx": sender},
        ).wait_recv()

    cells = cx * cy
    span = GROUP * slots
    high_index = lax.broadcasted_iota(jnp.int32, (cells, span), 0)
    low_index = lax.broadcasted_iota(jnp.int32, (nz, span), 0)

    def inject(half, first, last):
        def add_group(g, carry):
            senders = [(me + g * GROUP + j) % n for j in range(GROUP)]
            if half == 0:
                for sender in senders:

                    @pl.when(sender != me)
                    def _():
                        wait_traces(sender)

            block = jnp.concatenate([arrived[sender] for sender in senders], axis=1)
            cell = block[steps : steps + 1].astype(jnp.int32)
            high = (cell >> 7)
            low = cell & (LANES - 1)
            ones = jnp.where(high_index == high, 1.0, 0.0).astype(jnp.bfloat16)
            at_low = low_index == low
            coarse, fine = [], []
            for s in (2 * half, 2 * half + 1):
                value = block[s : s + 1]
                top = value.astype(jnp.bfloat16).astype(jnp.float32)
                coarse.append(jnp.where(at_low, top, 0.0).astype(jnp.bfloat16))
                fine.append(jnp.where(at_low, value - top, 0.0).astype(jnp.bfloat16))
            total = 0.0
            for part in (coarse, fine):
                total += lax.dot_general(
                    ones,
                    jnp.concatenate(part, axis=0),
                    (((1,), (1,)), ((), ())),
                    preferred_element_type=jnp.float32,
                )
            for j in range(2):
                sources[2 * half + j] += total[:, j * nz : (j + 1) * nz]
            return carry

        lax.fori_loop(first, last, add_group, 0)

    lane = lax.broadcasted_iota(jnp.int32, (1, nz), 1)
    up = [jnp.where(lane >= k, weights[k], 0.0) for k in range(1, 5)]
    down = [jnp.where(lane < nz - k, weights[k], 0.0) for k in range(1, 5)]

    def advance(s, first, last):
        def plane(x, carry):
            present = field[s, x + 4, 8 : 8 + cy]
            total = 3.0 * weights[0] * present
            for k in range(1, 5):
                pairs = field[s, x + 4 + k, 8 : 8 + cy] + field[s, x + 4 - k, 8 : 8 + cy]
                pairs += field[s, x + 4, 8 + k : 8 + k + cy]
                pairs += field[s, x + 4, 8 - k : 8 - k + cy]
                total += weights[k] * pairs
                total += up[k - 1] * pltpu.roll(present, k, 1)
                total += down[k - 1] * pltpu.roll(present, nz - k, 1)
            here = pl.ds(pl.multiple_of(x * cy, cy), cy)
            old = before_ref[x] if s == 0 else field[s - 1, x + 4, 8 : 8 + cy]
            following = 2.0 * present - old + vel_ref[x] * total
            if s == 0:
                sources[0, here] = following
                return carry
            following += sources[s, here]
            if s + 1 < steps:
                field[s + 1, x + 4, 8 : 8 + cy] = following
            else:
                final_ref[x] = following
                prior_ref[x] = present
            gradient_ref[x] += following * accel_ref[s, x].astype(jnp.float32)
            return carry

        lax.fori_loop(first, last, plane, 0)

    def begin(s, first, last):
        def plane(x, carry):
            here = pl.ds(pl.multiple_of(x * cy, cy), cy)
            following = sources[0, here]
            field[1, x + 4, 8 : 8 + cy] = following
            gradient_ref[x] = following * accel_ref[0, x].astype(jnp.float32)
            return carry

        lax.fori_loop(first, last, plane, 0)

    for s in range(1, steps):
        sources[s] = jnp.zeros((cells, nz), jnp.float32)
    for load in loads[4:]:
        load.wait()
    for way in range(4):
        wait_halo(0, way)
    advance(0, 0, cx)
    groups = n // GROUP
    inject(0, 0, groups)
    for s in range(steps):
        if s:
            for way in range(4):
                wait_halo(s, way)
        move = advance if s else begin
        move(s, 0, 4)
        if s + 1 < steps:
            send_halo(s + 1, 1)
        move(s, cx - 4, cx)
        if s + 1 < steps:
            send_halo(s + 1, 0)
        move(s, 4, cx - 4)
        if s + 1 < steps:
            send_halo(s + 1, 2)
            send_halo(s + 1, 3)
        if s == 0:
            inject(1, 0, groups // 2)
        if s == 1:
            inject(1, groups // 2, groups)

    def finish(j, carry):
        trace_copy((me + j) % n).wait_send()
        return carry

    lax.fori_loop(1, n, finish, 0)
    for s in range(steps):
        for way in range(4):

            @pl.when(has[way])
            def _():
                halo_copy(s, way).wait_send()


def write_out(final_ref, prior_ref, gradient_ref, final_hbm, prior_hbm, gradient_hbm, sem):
    pairs = ((final_ref, final_hbm), (prior_ref, prior_hbm), (gradient_ref, gradient_hbm))
    copies = [pltpu.make_async_copy(a, b, sem.at[i]) for i, (a, b) in enumerate(pairs)]
    for copy in copies:
        copy.start()
    for copy in copies:
        copy.wait()


def per_device(
    adjoint_now,
    adjoint_before,
    vel_coeff,
    forward_accel,
    residual,
    rec_cell,
    owner_list,
    trace_count,
):
    n = lax.axis_size("gx")
    steps, _, cx, cy, nz = forward_accel.shape
    traces = residual.shape[1]
    short = -owner_list.shape[1] % LANES
    lists = owner_list
    if short:
        lists = jnp.pad(owner_list, ((0, 0), (0, short)), constant_values=-1)
    slots = lists.shape[1]
    far = pl.BlockSpec(memory_space=pltpu.HBM)
    whole = pl.BlockSpec(memory_space=pltpu.VMEM)
    shape = jax.ShapeDtypeStruct((cx, cy, nz), jnp.float32)
    final, prior, gradient = pl.pallas_call(
        functools.partial(kernel, n),
        out_shape=(shape, shape, shape),
        in_specs=[far] * 7 + [pl.BlockSpec(memory_space=pltpu.SMEM)],
        out_specs=(whole, whole, whole),
        scratch_shapes=[
            pltpu.VMEM((cx, cy, nz), jnp.float32),
            pltpu.VMEM((cx, cy, nz), jnp.float32),
            pltpu.VMEM((steps, cx, cy, nz), forward_accel.dtype),
            pltpu.VMEM(residual.shape, jnp.float32),
            pltpu.VMEM((1, traces), jnp.int32),
            pltpu.VMEM(lists.shape, jnp.int32),
            pltpu.VMEM((ROWS, traces), jnp.float32),
            pltpu.VMEM((n, ROWS, slots), jnp.float32),
            pltpu.VMEM((n, ROWS, slots), jnp.float32),
            pltpu.VMEM((steps, cx + 8, cy + 16, nz), jnp.float32),
            pltpu.VMEM((steps, cx * cy, nz), jnp.float32),
            pltpu.SemaphoreType.DMA((steps, 4)),
            pltpu.SemaphoreType.DMA((steps, 4)),
            pltpu.SemaphoreType.DMA((n,)),
            pltpu.SemaphoreType.DMA((n,)),
            pltpu.SemaphoreType.DMA((7,)),
        ],
        compiler_params=pltpu.CompilerParams(
            collective_id=0, has_side_effects=True, vmem_limit_bytes=VMEM
        ),
    )(
        adjoint_now[0],
        adjoint_before[0],
        vel_coeff[0],
        forward_accel[:, 0],
        residual,
        rec_cell[None],
        lists,
        trace_count,
    )
    final, prior, gradient = pl.pallas_call(
        write_out,
        out_shape=(shape, shape, shape),
        in_specs=[far] * 3,
        out_specs=(far, far, far),
        scratch_shapes=[pltpu.SemaphoreType.DMA((3,))],
        compiler_params=pltpu.CompilerParams(vmem_limit_bytes=VMEM),
    )(final, prior, gradient)
    return final[None], prior[None], gradient[None]


def solution(mesh):
    in_specs = (
        P(("shot", "gx"), None, None, None),
        P(("shot", "gx"), None, None, None),
        P("gx", None, None, None),
        P("shot", "gx", None, None, None),
        P("shot", "gx"),
        P("gx"),
        P("gx", None),
        P(("shot", "gx")),
    )
    out_specs = (
        P(("shot", "gx"), None, None, None),
        P(("shot", "gx"), None, None, None),
        P(("shot", "gx"), None, None, None),
    )
    return jax.shard_map(
        per_device, mesh=mesh, in_specs=in_specs, out_specs=out_specs, check_vma=False
    )
```

```python
import functools

import jax
import jax.numpy as jnp
from jax import lax
from jax.experimental import pallas as pl
from jax.experimental.pallas import tpu as pltpu
from jax.sharding import PartitionSpec as P

PY = 4
LANES = 128
ROWS = 8
GROUP = 4
VMEM = 63 * 1024 * 1024

weights = (-205.0 / 72.0, 8.0 / 5.0, -1.0 / 5.0, 8.0 / 315.0, -1.0 / 560.0)


def kernel(
    n,
    now_hbm,
    before_hbm,
    vel_hbm,
    accel_hbm,
    residual_hbm,
    cell_hbm,
    list_hbm,
    count_ref,
    final_ref,
    prior_ref,
    gradient_ref,
    before_ref,
    vel_ref,
    accel_ref,
    residual_ref,
    cell_ref,
    list_ref,
    table,
    packed,
    arrived,
    field,
    sources,
    halo_send,
    halo_recv,
    trace_send,
    trace_recv,
    load_sem,
):
    steps, cx, cy, nz = accel_ref.shape
    traces = residual_ref.shape[1]
    slots = list_ref.shape[1]
    me = lax.axis_index("gx")
    spot = me % PY

    barrier = pltpu.get_barrier_semaphore()

    def greet(j, carry):
        pl.semaphore_signal(barrier, inc=1, device_id={"gx": (me + j) % n})
        return carry

    lax.fori_loop(1, n, greet, 0)

    loads = [
        pltpu.make_async_copy(there, here, load_sem.at[i])
        for i, (there, here) in enumerate(
            (
                (list_hbm, list_ref),
                (residual_hbm, residual_ref),
                (cell_hbm, cell_ref),
                (now_hbm, field.at[0, 4 : 4 + cx, 8 : 8 + cy]),
                (before_hbm, before_ref),
                (vel_hbm, vel_ref),
                (accel_hbm, accel_ref),
            )
        )
    ]
    for load in loads:
        load.start()

    has = (me + PY < n, me - PY >= 0, spot < PY - 1, spot > 0)
    gets = (has[1], has[0], has[3], has[2])
    target = ((me + PY) % n, (me - PY + n) % n, (me + 1) % n, (me - 1 + n) % n)
    inside_y = pl.ds(8, cy)
    inside_x = pl.ds(4, cx)
    source_of = (
        (pl.ds(cx, 4), inside_y),
        (pl.ds(4, 4), inside_y),
        (inside_x, pl.ds(cy + 4, 4)),
        (inside_x, pl.ds(8, 4)),
    )
    place_of = (
        (pl.ds(0, 4), inside_y),
        (pl.ds(cx + 4, 4), inside_y),
        (inside_x, pl.ds(4, 4)),
        (inside_x, pl.ds(cy + 8, 4)),
    )

    def halo_copy(s, way):
        return pltpu.make_async_remote_copy(
            src_ref=field.at[(s,) + source_of[way]],
            dst_ref=field.at[(s,) + place_of[way]],
            send_sem=halo_send.at[s, way],
            recv_sem=halo_recv.at[s, way],
            device_id={"gx": target[way]},
        )

    def send_halo(s, way):
        @pl.when(has[way])
        def _():
            halo_copy(s, way).start()

    def wait_halo(s, way):
        @pl.when(gets[way])
        def _():
            halo_copy(s, way).wait_recv()

    for way in range(4):

        @pl.when(jnp.logical_not(gets[way]))
        def _():
            for s in range(steps):
                place = field.at[(s,) + place_of[way]]
                place[...] = jnp.zeros(place.shape, jnp.float32)

    loads[3].wait()
    pl.semaphore_wait(barrier, n - 1)
    for way in range(4):
        send_halo(0, way)

    for load in loads[:3]:
        load.wait()
    table[0:steps] = residual_ref[...]
    table[steps : steps + 1] = cell_ref[...].astype(jnp.float32)
    table[steps + 1 :] = jnp.zeros((ROWS - steps - 1, traces), jnp.float32)
    used = slots // LANES * (steps + 1)
    if packed.shape[1] > used:
        packed[:, used:] = jnp.zeros((n, packed.shape[1] - used, LANES), jnp.float32)
    count = count_ref[0]
    row = lax.broadcasted_iota(jnp.int32, (ROWS, LANES), 0)

    def pack(t, carry):
        tile = list_ref[pl.ds(pl.multiple_of(t * ROWS, ROWS), ROWS)]
        for r in range(ROWS):
            for k in range(0, slots, LANES):
                listed = jnp.broadcast_to(tile[r : r + 1, k : k + LANES], (ROWS, LANES))
                high = listed >> 7
                low = listed & (LANES - 1)
                found = jnp.zeros((ROWS, LANES), jnp.float32)
                for h in range(traces // LANES):
                    taken = jnp.take_along_axis(
                        table[:, h * LANES : (h + 1) * LANES],
                        low,
                        axis=1,
                        mode="promise_in_bounds",
                    )
                    found = jnp.where(high == h, taken, found)
                kept = (listed < count) | (row >= steps)
                first = k // LANES * (steps + 1)
                packed[t * ROWS + r, first : first + steps + 1] = jnp.where(kept, found, 0.0)[
                    : steps + 1
                ]
        return carry

    lax.fori_loop(0, n // ROWS, pack, 0)

    def trace_copy(e):
        return pltpu.make_async_remote_copy(
            src_ref=packed.at[e],
            dst_ref=arrived.at[me],
            send_sem=trace_send.at[e],
            recv_sem=trace_recv.at[me],
            device_id={"gx": e},
        )

    def send_traces(j, carry):
        trace_copy((me + j) % n).start()
        return carry

    lax.fori_loop(1, n, send_traces, 0)
    arrived[me] = packed[me]

    def wait_traces(sender):
        pltpu.make_async_remote_copy(
            src_ref=packed.at[sender],
            dst_ref=arrived.at[sender],
            send_sem=trace_send.at[sender],
            recv_sem=trace_recv.at[sender],
            device_id={"gx": sender},
        ).wait_recv()

    cells = cx * cy
    span = GROUP * slots
    high_index = lax.broadcasted_iota(jnp.int32, (cells, span), 0)
    low_index = lax.broadcasted_iota(jnp.int32, (nz, span), 0)

    def inject(half, first, last):
        def add_group(g, carry):
            senders = [(me + g * GROUP + j) % n for j in range(GROUP)]
            if half == 0:
                for sender in senders:

                    @pl.when(sender != me)
                    def _():
                        wait_traces(sender)

            blocks = [arrived[sender] for sender in senders]

            def line(r):
                starts = range(r, slots // LANES * (steps + 1), steps + 1)
                return jnp.concatenate([b[i : i + 1] for b in blocks for i in starts], axis=1)

            cell = line(steps).astype(jnp.int32)
            high = (cell >> 7)
            low = cell & (LANES - 1)
            ones = jnp.where(high_index == high, 1.0, 0.0).astype(jnp.bfloat16)
            at_low = low_index == low
            coarse, fine = [], []
            for s in (2 * half, 2 * half + 1):
                value = line(s)
                top = value.astype(jnp.bfloat16).astype(jnp.float32)
                coarse.append(jnp.where(at_low, top, 0.0).astype(jnp.bfloat16))
                fine.append(jnp.where(at_low, value - top, 0.0).astype(jnp.bfloat16))
            total = 0.0
            for part in (coarse, fine):
                total += lax.dot_general(
                    ones,
                    jnp.concatenate(part, axis=0),
                    (((1,), (1,)), ((), ())),
                    preferred_element_type=jnp.float32,
                )
            for j in range(2):
                sources[2 * half + j] += total[:, j * nz : (j + 1) * nz]
            return carry

        lax.fori_loop(first, last, add_group, 0)

    lane = lax.broadcasted_iota(jnp.int32, (1, nz), 1)
    up = [jnp.where(lane >= k, weights[k], 0.0) for k in range(1, 5)]
    down = [jnp.where(lane < nz - k, weights[k], 0.0) for k in range(1, 5)]

    def advance(s, first, last):
        def plane(x, carry):
            present = field[s, x + 4, 8 : 8 + cy]
            total = 3.0 * weights[0] * present
            for k in range(1, 5):
                pairs = field[s, x + 4 + k, 8 : 8 + cy] + field[s, x + 4 - k, 8 : 8 + cy]
                pairs += field[s, x + 4, 8 + k : 8 + k + cy]
                pairs += field[s, x + 4, 8 - k : 8 - k + cy]
                total += weights[k] * pairs
                total += up[k - 1] * pltpu.roll(present, k, 1)
                total += down[k - 1] * pltpu.roll(present, nz - k, 1)
            here = pl.ds(pl.multiple_of(x * cy, cy), cy)
            old = before_ref[x] if s == 0 else field[s - 1, x + 4, 8 : 8 + cy]
            following = 2.0 * present - old + vel_ref[x] * total
            if s == 0:
                sources[0, here] = following
                return carry
            following += sources[s, here]
            if s + 1 < steps:
                field[s + 1, x + 4, 8 : 8 + cy] = following
            else:
                final_ref[x] = following
                prior_ref[x] = present
            gradient_ref[x] += following * accel_ref[s, x].astype(jnp.float32)
            return carry

        lax.fori_loop(first, last, plane, 0)

    def begin(s, first, last):
        def plane(x, carry):
            here = pl.ds(pl.multiple_of(x * cy, cy), cy)
            following = sources[0, here]
            field[1, x + 4, 8 : 8 + cy] = following
            gradient_ref[x] = following * accel_ref[0, x].astype(jnp.float32)
            return carry

        lax.fori_loop(first, last, plane, 0)

    for s in range(1, steps):
        sources[s] = jnp.zeros((cells, nz), jnp.float32)
    for load in loads[4:]:
        load.wait()
    for way in range(4):
        wait_halo(0, way)
    advance(0, 0, cx)
    groups = n // GROUP
    inject(0, 0, groups)
    for s in range(steps):
        if s:
            for way in range(4):
                wait_halo(s, way)
        move = advance if s else begin
        move(s, 0, 4)
        if s + 1 < steps:
            send_halo(s + 1, 1)
        move(s, cx - 4, cx)
        if s + 1 < steps:
            send_halo(s + 1, 0)
        move(s, 4, cx - 4)
        if s + 1 < steps:
            send_halo(s + 1, 2)
            send_halo(s + 1, 3)
        if s == 0:
            inject(1, 0, groups // 2)
        if s == 1:
            inject(1, groups // 2, groups)

    def finish(j, carry):
        trace_copy((me + j) % n).wait_send()
        return carry

    lax.fori_loop(1, n, finish, 0)
    for s in range(steps):
        for way in range(4):

            @pl.when(has[way])
            def _():
                halo_copy(s, way).wait_send()


def write_out(final_in, prior_in, gradient_in, final_out, prior_out, gradient_out, held, sem):
    ins = (final_in, prior_in, gradient_in)
    outs = (final_out, prior_out, gradient_out)
    loads = [pltpu.make_async_copy(ins[i], held.at[i], sem.at[0, i]) for i in range(3)]
    stores = [pltpu.make_async_copy(held.at[i], outs[i], sem.at[1, i]) for i in range(3)]
    for load in loads:
        load.start()
    for i in range(3):
        loads[i].wait()
        stores[i].start()
    for store in stores:
        store.wait()


def per_device(
    adjoint_now,
    adjoint_before,
    vel_coeff,
    forward_accel,
    residual,
    rec_cell,
    owner_list,
    trace_count,
):
    n = lax.axis_size("gx")
    steps, _, cx, cy, nz = forward_accel.shape
    traces = residual.shape[1]
    short = -owner_list.shape[1] % LANES
    lists = owner_list
    if short:
        lists = jnp.pad(owner_list, ((0, 0), (0, short)), constant_values=-1)
    slots = lists.shape[1]
    lines = -(-(slots // LANES * (steps + 1)) // ROWS) * ROWS
    far = pl.BlockSpec(memory_space=pltpu.HBM)
    whole = pl.BlockSpec(memory_space=pltpu.VMEM)
    shape = jax.ShapeDtypeStruct((cx, cy, nz), jnp.float32)
    final, prior, gradient = pl.pallas_call(
        functools.partial(kernel, n),
        out_shape=(shape, shape, shape),
        in_specs=[far] * 7 + [pl.BlockSpec(memory_space=pltpu.SMEM)],
        out_specs=(whole, whole, whole),
        scratch_shapes=[
            pltpu.VMEM((cx, cy, nz), jnp.float32),
            pltpu.VMEM((cx, cy, nz), jnp.float32),
            pltpu.VMEM((steps, cx, cy, nz), forward_accel.dtype),
            pltpu.VMEM(residual.shape, jnp.float32),
            pltpu.VMEM((1, traces), jnp.int32),
            pltpu.VMEM(lists.shape, jnp.int32),
            pltpu.VMEM((ROWS, traces), jnp.float32),
            pltpu.VMEM((n, lines, LANES), jnp.float32),
            pltpu.VMEM((n, lines, LANES), jnp.float32),
            pltpu.VMEM((steps, cx + 8, cy + 16, nz), jnp.float32),
            pltpu.VMEM((steps, cx * cy, nz), jnp.float32),
            pltpu.SemaphoreType.DMA((steps, 4)),
            pltpu.SemaphoreType.DMA((steps, 4)),
            pltpu.SemaphoreType.DMA((n,)),
            pltpu.SemaphoreType.DMA((n,)),
            pltpu.SemaphoreType.DMA((7,)),
        ],
        compiler_params=pltpu.CompilerParams(
            collective_id=0, has_side_effects=True, vmem_limit_bytes=VMEM
        ),
    )(
        adjoint_now[0],
        adjoint_before[0],
        vel_coeff[0],
        forward_accel[:, 0],
        residual,
        rec_cell[None],
        lists,
        trace_count,
    )
    final, prior, gradient = pl.pallas_call(
        write_out,
        out_shape=(shape, shape, shape),
        in_specs=[far] * 3,
        out_specs=(far, far, far),
        scratch_shapes=[pltpu.VMEM((3, cx, cy, nz), jnp.float32), pltpu.SemaphoreType.DMA((2, 3))],
        compiler_params=pltpu.CompilerParams(vmem_limit_bytes=VMEM),
    )(final, prior, gradient)
    return final[None], prior[None], gradient[None]


def solution(mesh):
    in_specs = (
        P(("shot", "gx"), None, None, None),
        P(("shot", "gx"), None, None, None),
        P("gx", None, None, None),
        P("shot", "gx", None, None, None),
        P("shot", "gx"),
        P("gx"),
        P("gx", None),
        P(("shot", "gx")),
    )
    out_specs = (
        P(("shot", "gx"), None, None, None),
        P(("shot", "gx"), None, None, None),
        P(("shot", "gx"), None, None, None),
    )
    return jax.shard_map(
        per_device, mesh=mesh, in_specs=in_specs, out_specs=out_specs, check_vma=False
    )
```

```python
import functools

import jax
import jax.numpy as jnp
from jax import lax
from jax.experimental import pallas as pl
from jax.experimental.pallas import tpu as pltpu
from jax.sharding import PartitionSpec as P

PY = 4
LANES = 128
ROWS = 8
GROUP = 4
VMEM = 63 * 1024 * 1024

weights = (-205.0 / 72.0, 8.0 / 5.0, -1.0 / 5.0, 8.0 / 315.0, -1.0 / 560.0)


def kernel(
    n,
    now_hbm,
    before_hbm,
    vel_hbm,
    accel_hbm,
    residual_hbm,
    cell_hbm,
    list_hbm,
    count_ref,
    final_ref,
    prior_ref,
    gradient_ref,
    before_ref,
    vel_ref,
    accel_ref,
    residual_ref,
    cell_ref,
    list_ref,
    table,
    packed,
    arrived,
    field,
    sources,
    halo_send,
    halo_recv,
    trace_send,
    trace_recv,
    load_sem,
):
    steps, cx, cy, nz = accel_ref.shape
    traces = residual_ref.shape[1]
    slots = list_ref.shape[1]
    me = lax.axis_index("gx")
    spot = me % PY

    barrier = pltpu.get_barrier_semaphore()

    def greet(j, carry):
        pl.semaphore_signal(barrier, inc=1, device_id={"gx": (me + j) % n})
        return carry

    lax.fori_loop(1, n, greet, 0)

    loads = [
        pltpu.make_async_copy(there, here, load_sem.at[i])
        for i, (there, here) in enumerate(
            (
                (list_hbm, list_ref),
                (residual_hbm, residual_ref),
                (cell_hbm, cell_ref),
                (now_hbm, field.at[0, 4 : 4 + cx, 8 : 8 + cy]),
                (before_hbm, before_ref),
                (vel_hbm, vel_ref),
                (accel_hbm, accel_ref),
            )
        )
    ]
    for load in loads:
        load.start()

    has = (me + PY < n, me - PY >= 0, spot < PY - 1, spot > 0)
    gets = (has[1], has[0], has[3], has[2])
    target = ((me + PY) % n, (me - PY + n) % n, (me + 1) % n, (me - 1 + n) % n)
    inside_y = pl.ds(8, cy)
    inside_x = pl.ds(4, cx)
    source_of = (
        (pl.ds(cx, 4), inside_y),
        (pl.ds(4, 4), inside_y),
        (inside_x, pl.ds(cy + 4, 4)),
        (inside_x, pl.ds(8, 4)),
    )
    place_of = (
        (pl.ds(0, 4), inside_y),
        (pl.ds(cx + 4, 4), inside_y),
        (inside_x, pl.ds(4, 4)),
        (inside_x, pl.ds(cy + 8, 4)),
    )

    def halo_copy(s, way):
        return pltpu.make_async_remote_copy(
            src_ref=field.at[(s,) + source_of[way]],
            dst_ref=field.at[(s,) + place_of[way]],
            send_sem=halo_send.at[s, way],
            recv_sem=halo_recv.at[s, way],
            device_id={"gx": target[way]},
        )

    def send_halo(s, way):
        @pl.when(has[way])
        def _():
            halo_copy(s, way).start()

    def wait_halo(s, way):
        @pl.when(gets[way])
        def _():
            halo_copy(s, way).wait_recv()

    for way in range(4):

        @pl.when(jnp.logical_not(gets[way]))
        def _():
            for s in range(steps):
                place = field.at[(s,) + place_of[way]]
                place[...] = jnp.zeros(place.shape, jnp.float32)

    loads[3].wait()
    pl.semaphore_wait(barrier, n - 1)
    for way in range(4):
        send_halo(0, way)

    for load in loads[:3]:
        load.wait()
    table[0:steps] = residual_ref[...]
    table[steps : steps + 1] = cell_ref[...].astype(jnp.float32)
    table[steps + 1 :] = jnp.zeros((ROWS - steps - 1, traces), jnp.float32)
    used = slots // LANES * (steps + 1)
    if packed.shape[1] > used:
        packed[:, used:] = jnp.zeros((n, packed.shape[1] - used, LANES), jnp.float32)
    count = count_ref[0]
    row = lax.broadcasted_iota(jnp.int32, (ROWS, LANES), 0)

    def pack(t, carry):
        tile = list_ref[pl.ds(pl.multiple_of(t * ROWS, ROWS), ROWS)]
        for r in range(ROWS):
            for k in range(0, slots, LANES):
                listed = jnp.broadcast_to(tile[r : r + 1, k : k + LANES], (ROWS, LANES))
                high = listed >> 7
                low = listed & (LANES - 1)
                found = jnp.zeros((ROWS, LANES), jnp.float32)
                for h in range(traces // LANES):
                    taken = jnp.take_along_axis(
                        table[:, h * LANES : (h + 1) * LANES],
                        low,
                        axis=1,
                        mode="promise_in_bounds",
                    )
                    found = jnp.where(high == h, taken, found)
                kept = (listed < count) | (row >= steps)
                first = k // LANES * (steps + 1)
                packed[t * ROWS + r, first : first + steps + 1] = jnp.where(kept, found, 0.0)[
                    : steps + 1
                ]
        return carry

    lax.fori_loop(0, n // ROWS, pack, 0)

    def trace_copy(e):
        return pltpu.make_async_remote_copy(
            src_ref=packed.at[e],
            dst_ref=arrived.at[me],
            send_sem=trace_send.at[e],
            recv_sem=trace_recv.at[me],
            device_id={"gx": e},
        )

    def send_traces(j, carry):
        trace_copy((me + n - j) % n).start()
        return carry

    lax.fori_loop(1, n, send_traces, 0)
    arrived[me] = packed[me]

    def wait_traces(sender):
        pltpu.make_async_remote_copy(
            src_ref=packed.at[sender],
            dst_ref=arrived.at[sender],
            send_sem=trace_send.at[sender],
            recv_sem=trace_recv.at[sender],
            device_id={"gx": sender},
        ).wait_recv()

    cells = cx * cy
    span = GROUP * slots
    high_index = lax.broadcasted_iota(jnp.int32, (cells, span), 0)
    low_index = lax.broadcasted_iota(jnp.int32, (nz, span), 0)

    def inject(half, first, last):
        def add_group(g, carry):
            senders = [(me + g * GROUP + j) % n for j in range(GROUP)]
            if half == 0:
                for sender in senders:

                    @pl.when(sender != me)
                    def _():
                        wait_traces(sender)

            blocks = [arrived[sender] for sender in senders]

            def line(r):
                starts = range(r, slots // LANES * (steps + 1), steps + 1)
                return jnp.concatenate([b[i : i + 1] for b in blocks for i in starts], axis=1)

            cell = line(steps).astype(jnp.int32)
            high = (cell >> 7)
            low = cell & (LANES - 1)
            ones = jnp.where(high_index == high, 1.0, 0.0).astype(jnp.bfloat16)
            at_low = low_index == low
            coarse, fine = [], []
            for s in (2 * half, 2 * half + 1):
                value = line(s)
                top = value.astype(jnp.bfloat16).astype(jnp.float32)
                coarse.append(jnp.where(at_low, top, 0.0).astype(jnp.bfloat16))
                fine.append(jnp.where(at_low, value - top, 0.0).astype(jnp.bfloat16))
            total = 0.0
            for part in (coarse, fine):
                total += lax.dot_general(
                    ones,
                    jnp.concatenate(part, axis=0),
                    (((1,), (1,)), ((), ())),
                    preferred_element_type=jnp.float32,
                )
            for j in range(2):
                sources[2 * half + j] += total[:, j * nz : (j + 1) * nz]
            return carry

        lax.fori_loop(first, last, add_group, 0)

    lane = lax.broadcasted_iota(jnp.int32, (1, nz), 1)
    up = [jnp.where(lane >= k, weights[k], 0.0) for k in range(1, 5)]
    down = [jnp.where(lane < nz - k, weights[k], 0.0) for k in range(1, 5)]

    def advance(s, first, last):
        def plane(x, carry):
            present = field[s, x + 4, 8 : 8 + cy]
            total = 3.0 * weights[0] * present
            for k in range(1, 5):
                pairs = field[s, x + 4 + k, 8 : 8 + cy] + field[s, x + 4 - k, 8 : 8 + cy]
                pairs += field[s, x + 4, 8 + k : 8 + k + cy]
                pairs += field[s, x + 4, 8 - k : 8 - k + cy]
                total += weights[k] * pairs
                total += up[k - 1] * pltpu.roll(present, k, 1)
                total += down[k - 1] * pltpu.roll(present, nz - k, 1)
            here = pl.ds(pl.multiple_of(x * cy, cy), cy)
            old = before_ref[x] if s == 0 else field[s - 1, x + 4, 8 : 8 + cy]
            following = 2.0 * present - old + vel_ref[x] * total
            if s == 0:
                sources[0, here] = following
                return carry
            following += sources[s, here]
            if s + 1 < steps:
                field[s + 1, x + 4, 8 : 8 + cy] = following
            else:
                final_ref[x] = following
                prior_ref[x] = present
            gradient_ref[x] += following * accel_ref[s, x].astype(jnp.float32)
            return carry

        lax.fori_loop(first, last, plane, 0, unroll=4)

    def begin(s, first, last):
        def plane(x, carry):
            here = pl.ds(pl.multiple_of(x * cy, cy), cy)
            following = sources[0, here]
            field[1, x + 4, 8 : 8 + cy] = following
            gradient_ref[x] = following * accel_ref[0, x].astype(jnp.float32)
            return carry

        lax.fori_loop(first, last, plane, 0, unroll=4)

    for s in range(1, steps):
        sources[s] = jnp.zeros((cells, nz), jnp.float32)
    for load in loads[4:]:
        load.wait()
    for way in range(4):
        wait_halo(0, way)
    advance(0, 0, cx)
    groups = n // GROUP
    inject(0, 0, groups)
    for s in range(steps):
        if s:
            for way in range(4):
                wait_halo(s, way)
        move = advance if s else begin
        move(s, 0, 4)
        if s + 1 < steps:
            send_halo(s + 1, 1)
        move(s, cx - 4, cx)
        if s + 1 < steps:
            send_halo(s + 1, 0)
        move(s, 4, cx - 4)
        if s + 1 < steps:
            send_halo(s + 1, 2)
            send_halo(s + 1, 3)
        if s == 0:
            inject(1, 0, groups // 2)
        if s == 1:
            inject(1, groups // 2, groups)

    def finish(j, carry):
        trace_copy((me + j) % n).wait_send()
        return carry

    lax.fori_loop(1, n, finish, 0)
    for s in range(steps):
        for way in range(4):

            @pl.when(has[way])
            def _():
                halo_copy(s, way).wait_send()


def write_out(final_in, prior_in, gradient_in, final_out, prior_out, gradient_out, held, sem):
    ins = (final_in, prior_in, gradient_in)
    outs = (final_out, prior_out, gradient_out)
    loads = [pltpu.make_async_copy(ins[i], held.at[i], sem.at[0, i]) for i in range(3)]
    stores = [pltpu.make_async_copy(held.at[i], outs[i], sem.at[1, i]) for i in range(3)]
    for load in loads:
        load.start()
    for i in range(3):
        loads[i].wait()
        stores[i].start()
    for store in stores:
        store.wait()


def per_device(
    adjoint_now,
    adjoint_before,
    vel_coeff,
    forward_accel,
    residual,
    rec_cell,
    owner_list,
    trace_count,
):
    n = lax.axis_size("gx")
    steps, _, cx, cy, nz = forward_accel.shape
    traces = residual.shape[1]
    short = -owner_list.shape[1] % LANES
    lists = owner_list
    if short:
        lists = jnp.pad(owner_list, ((0, 0), (0, short)), constant_values=-1)
    slots = lists.shape[1]
    lines = -(-(slots // LANES * (steps + 1)) // ROWS) * ROWS
    far = pl.BlockSpec(memory_space=pltpu.HBM)
    whole = pl.BlockSpec(memory_space=pltpu.VMEM)
    shape = jax.ShapeDtypeStruct((cx, cy, nz), jnp.float32)
    final, prior, gradient = pl.pallas_call(
        functools.partial(kernel, n),
        out_shape=(shape, shape, shape),
        in_specs=[far] * 7 + [pl.BlockSpec(memory_space=pltpu.SMEM)],
        out_specs=(whole, whole, whole),
        scratch_shapes=[
            pltpu.VMEM((cx, cy, nz), jnp.float32),
            pltpu.VMEM((cx, cy, nz), jnp.float32),
            pltpu.VMEM((steps, cx, cy, nz), forward_accel.dtype),
            pltpu.VMEM(residual.shape, jnp.float32),
            pltpu.VMEM((1, traces), jnp.int32),
            pltpu.VMEM(lists.shape, jnp.int32),
            pltpu.VMEM((ROWS, traces), jnp.float32),
            pltpu.VMEM((n, lines, LANES), jnp.float32),
            pltpu.VMEM((n, lines, LANES), jnp.float32),
            pltpu.VMEM((steps, cx + 8, cy + 16, nz), jnp.float32),
            pltpu.VMEM((steps, cx * cy, nz), jnp.float32),
            pltpu.SemaphoreType.DMA((steps, 4)),
            pltpu.SemaphoreType.DMA((steps, 4)),
            pltpu.SemaphoreType.DMA((n,)),
            pltpu.SemaphoreType.DMA((n,)),
            pltpu.SemaphoreType.DMA((7,)),
        ],
        compiler_params=pltpu.CompilerParams(
            collective_id=0, has_side_effects=True, vmem_limit_bytes=VMEM
        ),
    )(
        adjoint_now[0],
        adjoint_before[0],
        vel_coeff[0],
        forward_accel[:, 0],
        residual,
        rec_cell[None],
        lists,
        trace_count,
    )
    final, prior, gradient = pl.pallas_call(
        write_out,
        out_shape=(shape, shape, shape),
        in_specs=[far] * 3,
        out_specs=(far, far, far),
        scratch_shapes=[pltpu.VMEM((3, cx, cy, nz), jnp.float32), pltpu.SemaphoreType.DMA((2, 3))],
        compiler_params=pltpu.CompilerParams(vmem_limit_bytes=VMEM),
    )(final, prior, gradient)
    return final[None], prior[None], gradient[None]


def solution(mesh):
    in_specs = (
        P(("shot", "gx"), None, None, None),
        P(("shot", "gx"), None, None, None),
        P("gx", None, None, None),
        P("shot", "gx", None, None, None),
        P("shot", "gx"),
        P("gx"),
        P("gx", None),
        P(("shot", "gx")),
    )
    out_specs = (
        P(("shot", "gx"), None, None, None),
        P(("shot", "gx"), None, None, None),
        P(("shot", "gx"), None, None, None),
    )
    return jax.shard_map(
        per_device, mesh=mesh, in_specs=in_specs, out_specs=out_specs, check_vma=False
    )
```

```python
import functools

import jax
import jax.numpy as jnp
from jax import lax
from jax.experimental import pallas as pl
from jax.experimental.pallas import tpu as pltpu
from jax.sharding import PartitionSpec as P

PY = 4
LANES = 128
ROWS = 8
GROUP = 4
VMEM = 63 * 1024 * 1024

weights = (-205.0 / 72.0, 8.0 / 5.0, -1.0 / 5.0, 8.0 / 315.0, -1.0 / 560.0)


def kernel(
    n,
    now_hbm,
    before_hbm,
    vel_hbm,
    accel_hbm,
    residual_hbm,
    cell_hbm,
    list_hbm,
    count_ref,
    final_ref,
    prior_ref,
    gradient_ref,
    before_ref,
    vel_ref,
    accel_ref,
    residual_ref,
    cell_ref,
    list_ref,
    table,
    packed,
    arrived,
    field,
    sources,
    halo_send,
    halo_recv,
    trace_send,
    trace_recv,
    load_sem,
):
    steps, cx, cy, nz = accel_ref.shape
    traces = residual_ref.shape[1]
    slots = list_ref.shape[1]
    me = lax.axis_index("gx")
    spot = me % PY

    barrier = pltpu.get_barrier_semaphore()

    def greet(j, carry):
        pl.semaphore_signal(barrier, inc=1, device_id={"gx": (me + j) % n})
        return carry

    lax.fori_loop(1, n, greet, 0)

    loads = [
        pltpu.make_async_copy(there, here, load_sem.at[i])
        for i, (there, here) in enumerate(
            (
                (list_hbm, list_ref),
                (residual_hbm, residual_ref),
                (cell_hbm, cell_ref),
                (now_hbm, field.at[0, 4 : 4 + cx, 8 : 8 + cy]),
                (before_hbm, before_ref),
                (vel_hbm, vel_ref),
                (accel_hbm, accel_ref),
            )
        )
    ]
    for load in loads:
        load.start()

    has = (me + PY < n, me - PY >= 0, spot < PY - 1, spot > 0)
    gets = (has[1], has[0], has[3], has[2])
    target = ((me + PY) % n, (me - PY + n) % n, (me + 1) % n, (me - 1 + n) % n)
    inside_y = pl.ds(8, cy)
    inside_x = pl.ds(4, cx)
    source_of = (
        (pl.ds(cx, 4), inside_y),
        (pl.ds(4, 4), inside_y),
        (inside_x, pl.ds(cy + 4, 4)),
        (inside_x, pl.ds(8, 4)),
    )
    place_of = (
        (pl.ds(0, 4), inside_y),
        (pl.ds(cx + 4, 4), inside_y),
        (inside_x, pl.ds(4, 4)),
        (inside_x, pl.ds(cy + 8, 4)),
    )

    def halo_copy(s, way):
        return pltpu.make_async_remote_copy(
            src_ref=field.at[(s,) + source_of[way]],
            dst_ref=field.at[(s,) + place_of[way]],
            send_sem=halo_send.at[s, way],
            recv_sem=halo_recv.at[s, way],
            device_id={"gx": target[way]},
        )

    def send_halo(s, way):
        @pl.when(has[way])
        def _():
            halo_copy(s, way).start()

    def wait_halo(s, way):
        @pl.when(gets[way])
        def _():
            halo_copy(s, way).wait_recv()

    for way in range(4):

        @pl.when(jnp.logical_not(gets[way]))
        def _():
            for s in range(steps):
                place = field.at[(s,) + place_of[way]]
                place[...] = jnp.zeros(place.shape, jnp.float32)

    loads[3].wait()
    pl.semaphore_wait(barrier, n - 1)
    for way in range(4):
        send_halo(0, way)

    for load in loads[:3]:
        load.wait()
    table[0:steps] = residual_ref[...]
    table[steps : steps + 1] = cell_ref[...].astype(jnp.float32)
    table[steps + 1 :] = jnp.zeros((ROWS - steps - 1, traces), jnp.float32)
    used = slots // LANES * (steps + 1)
    if packed.shape[1] > used:
        packed[:, used:] = jnp.zeros((n, packed.shape[1] - used, LANES), jnp.float32)
    count = count_ref[0]
    row = lax.broadcasted_iota(jnp.int32, (ROWS, LANES), 0)

    def pack(t, carry):
        tile = list_ref[pl.ds(pl.multiple_of(t * ROWS, ROWS), ROWS)]
        for r in range(ROWS):
            for k in range(0, slots, LANES):
                listed = jnp.broadcast_to(tile[r : r + 1, k : k + LANES], (ROWS, LANES))
                high = listed >> 7
                low = listed & (LANES - 1)
                found = jnp.zeros((ROWS, LANES), jnp.float32)
                for h in range(traces // LANES):
                    taken = jnp.take_along_axis(
                        table[:, h * LANES : (h + 1) * LANES],
                        low,
                        axis=1,
                        mode="promise_in_bounds",
                    )
                    found = jnp.where(high == h, taken, found)
                kept = (listed < count) | (row >= steps)
                first = k // LANES * (steps + 1)
                packed[t * ROWS + r, first : first + steps + 1] = jnp.where(kept, found, 0.0)[
                    : steps + 1
                ]
        return carry

    lax.fori_loop(0, n // ROWS, pack, 0)

    def trace_copy(e):
        return pltpu.make_async_remote_copy(
            src_ref=packed.at[e],
            dst_ref=arrived.at[me],
            send_sem=trace_send.at[e],
            recv_sem=trace_recv.at[me],
            device_id={"gx": e},
        )

    def send_traces(j, carry):
        trace_copy((me + n - j) % n).start()
        return carry

    lax.fori_loop(1, n, send_traces, 0)
    arrived[me] = packed[me]

    def wait_traces(sender):
        pltpu.make_async_remote_copy(
            src_ref=packed.at[sender],
            dst_ref=arrived.at[sender],
            send_sem=trace_send.at[sender],
            recv_sem=trace_recv.at[sender],
            device_id={"gx": sender},
        ).wait_recv()

    cells = cx * cy
    span = GROUP * slots
    high_index = lax.broadcasted_iota(jnp.int32, (cells, span), 0)
    low_index = lax.broadcasted_iota(jnp.int32, (nz, span), 0)

    def inject(half, first, last):
        def add_group(g, carry):
            senders = [(me + g * GROUP + j) % n for j in range(GROUP)]
            if half == 0:
                for sender in senders:

                    @pl.when(sender != me)
                    def _():
                        wait_traces(sender)

            blocks = [arrived[sender] for sender in senders]

            def line(r):
                starts = range(r, slots // LANES * (steps + 1), steps + 1)
                return jnp.concatenate([b[i : i + 1] for b in blocks for i in starts], axis=1)

            cell = line(steps).astype(jnp.int32)
            high = (cell >> 7)
            low = cell & (LANES - 1)
            ones = jnp.where(high_index == high, 1.0, 0.0).astype(jnp.bfloat16)
            at_low = low_index == low
            coarse, fine = [], []
            for s in (2 * half, 2 * half + 1):
                value = line(s)
                top = value.astype(jnp.bfloat16).astype(jnp.float32)
                coarse.append(jnp.where(at_low, top, 0.0).astype(jnp.bfloat16))
                fine.append(jnp.where(at_low, value - top, 0.0).astype(jnp.bfloat16))
            total = 0.0
            for part in (coarse, fine):
                total += lax.dot_general(
                    ones,
                    jnp.concatenate(part, axis=0),
                    (((1,), (1,)), ((), ())),
                    preferred_element_type=jnp.float32,
                )
            for j in range(2):
                sources[2 * half + j] += total[:, j * nz : (j + 1) * nz]
            return carry

        lax.fori_loop(first, last, add_group, 0)

    lane = lax.broadcasted_iota(jnp.int32, (1, nz), 1)
    up = [jnp.where(lane >= k, weights[k], 0.0) for k in range(1, 5)]
    down = [jnp.where(lane < nz - k, weights[k], 0.0) for k in range(1, 5)]

    def advance(s, first, last):
        def plane(x, carry):
            present = field[s, x + 4, 8 : 8 + cy]
            total = 3.0 * weights[0] * present
            for k in range(1, 5):
                pairs = field[s, x + 4 + k, 8 : 8 + cy] + field[s, x + 4 - k, 8 : 8 + cy]
                pairs += field[s, x + 4, 8 + k : 8 + k + cy]
                pairs += field[s, x + 4, 8 - k : 8 - k + cy]
                total += weights[k] * pairs
                total += up[k - 1] * pltpu.roll(present, k, 1)
                total += down[k - 1] * pltpu.roll(present, nz - k, 1)
            here = pl.ds(pl.multiple_of(x * cy, cy), cy)
            old = before_ref[x] if s == 0 else field[s - 1, x + 4, 8 : 8 + cy]
            following = 2.0 * present - old + vel_ref[x] * total
            if s == 0:
                sources[0, here] = following
                return carry
            following += sources[s, here]
            if s + 1 < steps:
                field[s + 1, x + 4, 8 : 8 + cy] = following
            else:
                final_ref[x] = following
                prior_ref[x] = present
            gradient_ref[x] += following * accel_ref[s, x].astype(jnp.float32)
            return carry

        lax.fori_loop(first, last, plane, 0, unroll=True)

    def begin(s, first, last):
        def plane(x, carry):
            here = pl.ds(pl.multiple_of(x * cy, cy), cy)
            following = sources[0, here]
            field[1, x + 4, 8 : 8 + cy] = following
            gradient_ref[x] = following * accel_ref[0, x].astype(jnp.float32)
            return carry

        lax.fori_loop(first, last, plane, 0, unroll=True)

    for s in range(1, steps):
        sources[s] = jnp.zeros((cells, nz), jnp.float32)
    for load in loads[4:]:
        load.wait()
    for way in range(4):
        wait_halo(0, way)
    advance(0, 0, cx)
    groups = n // GROUP
    inject(0, 0, groups)
    for s in range(steps):
        if s:
            for way in (0, 2, 3):
                wait_halo(s, way)
        move = advance if s else begin
        move(s, 0, 4)
        if s + 1 < steps:
            send_halo(s + 1, 1)
        if s:
            wait_halo(s, 1)
        move(s, cx - 4, cx)
        if s + 1 < steps:
            send_halo(s + 1, 0)
        move(s, 4, cx - 4)
        if s + 1 < steps:
            send_halo(s + 1, 2)
            send_halo(s + 1, 3)
        if s == 0:
            inject(1, 0, groups // 2)
        if s == 1:
            inject(1, groups // 2, groups)

    def finish(j, carry):
        trace_copy((me + j) % n).wait_send()
        return carry

    lax.fori_loop(1, n, finish, 0)
    for s in range(steps):
        for way in range(4):

            @pl.when(has[way])
            def _():
                halo_copy(s, way).wait_send()


def write_out(final_in, prior_in, gradient_in, final_out, prior_out, gradient_out, held, sem):
    ins = (final_in, prior_in, gradient_in)
    outs = (final_out, prior_out, gradient_out)
    loads = [pltpu.make_async_copy(ins[i], held.at[i], sem.at[0, i]) for i in range(3)]
    stores = [pltpu.make_async_copy(held.at[i], outs[i], sem.at[1, i]) for i in range(3)]
    for load in loads:
        load.start()
    for i in range(3):
        loads[i].wait()
        stores[i].start()
    for store in stores:
        store.wait()


def per_device(
    adjoint_now,
    adjoint_before,
    vel_coeff,
    forward_accel,
    residual,
    rec_cell,
    owner_list,
    trace_count,
):
    n = lax.axis_size("gx")
    steps, _, cx, cy, nz = forward_accel.shape
    traces = residual.shape[1]
    short = -owner_list.shape[1] % LANES
    lists = owner_list
    if short:
        lists = jnp.pad(owner_list, ((0, 0), (0, short)), constant_values=-1)
    slots = lists.shape[1]
    lines = -(-(slots // LANES * (steps + 1)) // ROWS) * ROWS
    far = pl.BlockSpec(memory_space=pltpu.HBM)
    whole = pl.BlockSpec(memory_space=pltpu.VMEM)
    shape = jax.ShapeDtypeStruct((cx, cy, nz), jnp.float32)
    final, prior, gradient = pl.pallas_call(
        functools.partial(kernel, n),
        out_shape=(shape, shape, shape),
        in_specs=[far] * 7 + [pl.BlockSpec(memory_space=pltpu.SMEM)],
        out_specs=(whole, whole, whole),
        scratch_shapes=[
            pltpu.VMEM((cx, cy, nz), jnp.float32),
            pltpu.VMEM((cx, cy, nz), jnp.float32),
            pltpu.VMEM((steps, cx, cy, nz), forward_accel.dtype),
            pltpu.VMEM(residual.shape, jnp.float32),
            pltpu.VMEM((1, traces), jnp.int32),
            pltpu.VMEM(lists.shape, jnp.int32),
            pltpu.VMEM((ROWS, traces), jnp.float32),
            pltpu.VMEM((n, lines, LANES), jnp.float32),
            pltpu.VMEM((n, lines, LANES), jnp.float32),
            pltpu.VMEM((steps, cx + 8, cy + 16, nz), jnp.float32),
            pltpu.VMEM((steps, cx * cy, nz), jnp.float32),
            pltpu.SemaphoreType.DMA((steps, 4)),
            pltpu.SemaphoreType.DMA((steps, 4)),
            pltpu.SemaphoreType.DMA((n,)),
            pltpu.SemaphoreType.DMA((n,)),
            pltpu.SemaphoreType.DMA((7,)),
        ],
        compiler_params=pltpu.CompilerParams(
            collective_id=0, has_side_effects=True, vmem_limit_bytes=VMEM
        ),
    )(
        adjoint_now[0],
        adjoint_before[0],
        vel_coeff[0],
        forward_accel[:, 0],
        residual,
        rec_cell[None],
        lists,
        trace_count,
    )
    final, prior, gradient = pl.pallas_call(
        write_out,
        out_shape=(shape, shape, shape),
        in_specs=[far] * 3,
        out_specs=(far, far, far),
        scratch_shapes=[pltpu.VMEM((3, cx, cy, nz), jnp.float32), pltpu.SemaphoreType.DMA((2, 3))],
        compiler_params=pltpu.CompilerParams(vmem_limit_bytes=VMEM),
    )(final, prior, gradient)
    return final[None], prior[None], gradient[None]


def solution(mesh):
    in_specs = (
        P(("shot", "gx"), None, None, None),
        P(("shot", "gx"), None, None, None),
        P("gx", None, None, None),
        P("shot", "gx", None, None, None),
        P("shot", "gx"),
        P("gx"),
        P("gx", None),
        P(("shot", "gx")),
    )
    out_specs = (
        P(("shot", "gx"), None, None, None),
        P(("shot", "gx"), None, None, None),
        P(("shot", "gx"), None, None, None),
    )
    return jax.shard_map(
        per_device, mesh=mesh, in_specs=in_specs, out_specs=out_specs, check_vma=False
    )
```
